256 devices in a mesh: blk: 32 (over z_hi, y, core), head: 8 (over x, z_lo).
Axes of the slice: x: 4, y: 4, z: 8 (z_hi: 4, z_lo: 2; z = z_hi * 2 + z_lo), core: 2. Of those that a mesh axis runs over, the one named last changes fastest.
Arguments:
- tokens: bfloat16 [64, 256, 5120], P('blk', 'head'), may hold values from -6 to 6
- span_pos: int32 [64], replicated, may hold values from 0 to 63, each once
- w_query: bfloat16 [5120, 8192], P('blk', 'head'), may hold values from -0.05660047 to 0.05660047
- key_projection: bfloat16 [5120, 1024], P('blk', 'head'), may hold values from -0.05660047 to 0.05660047
- value_projection: bfloat16 [5120, 1024], P('blk', 'head'), may hold values from -0.078125 to 0.078125
- query_gain: float32 [128], replicated, may hold values from 0.3 to 4
- key_gain: float32 [128], replicated, may hold values from 0.3 to 4
Outputs:
- partial_out: float32 [64, 64, 256, 128], P('head', 'blk')
- log_sum: float32 [64, 64, 256], P('head', 'blk')
The draws below stay inside these ranges and needn't reach their ends.
Inputs may be any that keep to these rules, and one draw needn't show every extreme that they name: `span_pos`: each of 0 to 63 once.
All inputs are finite; a program needn't handle non-finite values.
Results may differ from the reference program's by a relative error of at most 0.008.
Values may be sent and summed in bfloat16 or wider, within the bound.
A program may use at most 128 MiB of HBM per device.

```python
import math
import jax
import jax.numpy as jnp
from jax import lax

MODEL_DIM = 5120
QUERY_HEAD_COUNT = 64
KEY_VALUE_HEADS = 8
HEAD_SIZE = 128
BLOCK_TOKENS = 256
CYCLE_STEP_COUNT = 3
SEQUENCE_BLOCKS = 64
N_BLK = 32


def key_base(key):
    random_root_key = jax.random.fold_in(key, 11)
    sampled_values = jax.random.normal(random_root_key, (MODEL_DIM, KEY_VALUE_HEADS, HEAD_SIZE), jnp.float32)
    return jnp.clip(sampled_values, -4.0, 4.0) * MODEL_DIM ** (-0.5)


def draw_key_projection(key, part):
    common_rows = key_base(key)
    return common_rows.reshape(MODEL_DIM, KEY_VALUE_HEADS * HEAD_SIZE).astype(jnp.bfloat16)


def draw_w_query(key, part):
    own_key = jax.random.fold_in(key, 5)
    random_draw_key = jax.random.fold_in(own_key, 0)
    random_draws = jnp.clip(jax.random.normal(random_draw_key, (MODEL_DIM, KEY_VALUE_HEADS, QUERY_HEAD_COUNT // KEY_VALUE_HEADS, HEAD_SIZE), jnp.float32), -4.0, 4.0) * MODEL_DIM ** (-0.5)
    mixed = random_draws
    return mixed.reshape(MODEL_DIM, QUERY_HEAD_COUNT * HEAD_SIZE).astype(jnp.bfloat16)


def draw_tokens(key, part):
    key = jax.random.fold_in(key, 7)
    random_draw_key = jax.random.fold_in(key, 0)
    random_draws = jax.random.normal(random_draw_key, (SEQUENCE_BLOCKS, BLOCK_TOKENS, MODEL_DIM), jnp.float32)
    result = jnp.clip(random_draws, -6.0, 6.0)
    return result.astype(jnp.bfloat16)


def gain_values(key):
    return jnp.exp(jax.random.uniform(key, (HEAD_SIZE,), jnp.float32, math.log(0.3), math.log(3.0)))


def draw_query_gain(key, part):
    key = jax.random.fold_in(key, 13)
    return gain_values(key)


def draw_key_gain(key, part):
    key = jax.random.fold_in(key, 17)
    return gain_values(key)


def block_levels(key, extent, pieces, least, largest):
    factor_of = 1.0
    for dim, shards_of in pieces:
        heights = jax.random.uniform(jax.random.fold_in(jax.random.fold_in(key, 6), dim), (shards_of,), jnp.float32, least / len(pieces), largest / len(pieces))
        factor_of = factor_of * jnp.repeat(jnp.exp(heights), extent[dim] // shards_of).reshape((-1,) + (1,) * (len(extent) - 1 - dim))
    return factor_of


def scatter_about(stream_key, shape, scale, bound, pieces=(), held_as=jnp.bfloat16):
    drawn = jax.random.normal(stream_key, shape, jnp.float32) * scale
    if len(pieces) > 0:
        drawn = block_levels(stream_key, shape, pieces, -0.22, 0.18) * drawn
    return jnp.clip(drawn, min=-bound, max=bound).astype(held_as)


def setup_inputs(seed: int = 0) -> dict:
    key_of = jax.random.split(jax.random.key(seed), 8)
    return {
        "tokens": draw_tokens(jax.random.fold_in(key_of[7], 71), 0),
        "span_pos": jax.random.permutation(key_of[1], SEQUENCE_BLOCKS).astype(jnp.int32),
        "w_query": draw_w_query(jax.random.fold_in(key_of[7], 71), 0),
        "key_projection": draw_key_projection(jax.random.fold_in(key_of[7], 71), 0),
        "value_projection": scatter_about(key_of[4], (MODEL_DIM, KEY_VALUE_HEADS * HEAD_SIZE), MODEL_DIM ** -0.5, 0.078125, ((0, 32), (1, 8))),
        "query_gain": draw_query_gain(jax.random.fold_in(key_of[7], 71), 0),
        "key_gain": draw_key_gain(jax.random.fold_in(key_of[7], 71), 0),
    }


ROPE_BASE = 1000000.0
EPSILON = 1e-06
NEGATIVE = -1e+30

def norm_rotate(value_rows, gain_vector, position):
    head_width = value_rows.shape[-1]
    half_width = head_width // 2
    mean_sq = lax.optimization_barrier(jnp.mean(value_rows * value_rows, axis=-1, keepdims=True))
    normed = value_rows * lax.rsqrt(mean_sq + EPSILON) * gain_vector
    frequency = ROPE_BASE ** (-(jnp.arange(half_width, dtype=jnp.float32) * 2.0 / head_width))
    angles = position.astype(jnp.float32)[:, None] * frequency[None, :]
    cosine = jnp.cos(angles)[:, None, :]
    sine_part = jnp.sin(angles)[:, None, :]
    first_half = normed[..., :half_width]
    second = normed[..., half_width:]
    return jnp.concatenate([first_half * cosine - second * sine_part, second * cosine + first_half * sine_part], axis=-1)

def reference(tokens, span_pos, w_query, key_projection, value_projection, query_gain, key_gain):
    group_count = QUERY_HEAD_COUNT // KEY_VALUE_HEADS
    row_index = jnp.arange(BLOCK_TOKENS, dtype=jnp.int32)
    positions = (span_pos[:, None] * BLOCK_TOKENS + row_index[None, :]).reshape(SEQUENCE_BLOCKS * BLOCK_TOKENS)
    flat_rows = tokens.reshape(SEQUENCE_BLOCKS * BLOCK_TOKENS, MODEL_DIM)
    every_key_row = jnp.dot(flat_rows, key_projection, preferred_element_type=jnp.float32).reshape(SEQUENCE_BLOCKS * BLOCK_TOKENS, KEY_VALUE_HEADS, HEAD_SIZE)
    every_key_row = norm_rotate(every_key_row, key_gain, positions).astype(jnp.bfloat16)
    every_value_row = jnp.dot(flat_rows, value_projection, preferred_element_type=jnp.float32).astype(jnp.bfloat16)
    every_value_row = every_value_row.reshape(SEQUENCE_BLOCKS * BLOCK_TOKENS, KEY_VALUE_HEADS, HEAD_SIZE)
    grouped_key_rows = every_key_row.reshape(N_BLK, 2 * BLOCK_TOKENS, KEY_VALUE_HEADS, HEAD_SIZE)
    grouped_value_rows = every_value_row.reshape(N_BLK, 2 * BLOCK_TOKENS, KEY_VALUE_HEADS, HEAD_SIZE)
    pos_group = positions.reshape(N_BLK, 2 * BLOCK_TOKENS)
    scale = HEAD_SIZE ** (-0.5)

    def one_group(cycle_index):
        start = (cycle_index * 2 * BLOCK_TOKENS).astype(jnp.int32)
        rows = lax.dynamic_slice_in_dim(flat_rows, start, 2 * BLOCK_TOKENS, 0)
        query_pos = lax.dynamic_slice_in_dim(positions, start, 2 * BLOCK_TOKENS, 0)
        query_rows = jnp.dot(rows, w_query, preferred_element_type=jnp.float32).reshape(2 * BLOCK_TOKENS, QUERY_HEAD_COUNT, HEAD_SIZE)
        query_rows = norm_rotate(query_rows, query_gain, query_pos).astype(jnp.bfloat16)
        query_rows = query_rows.reshape(2 * BLOCK_TOKENS, KEY_VALUE_HEADS, group_count, HEAD_SIZE)
        source_blocks = (cycle_index - jnp.arange(CYCLE_STEP_COUNT + 1, dtype=jnp.int32)) % N_BLK
        key_rows = grouped_key_rows[source_blocks].reshape((CYCLE_STEP_COUNT + 1) * 2 * BLOCK_TOKENS, KEY_VALUE_HEADS, HEAD_SIZE)
        value_rows = grouped_value_rows[source_blocks].reshape((CYCLE_STEP_COUNT + 1) * 2 * BLOCK_TOKENS, KEY_VALUE_HEADS, HEAD_SIZE)
        key_pos = pos_group[source_blocks].reshape((CYCLE_STEP_COUNT + 1) * 2 * BLOCK_TOKENS)
        scores = jnp.einsum('qhgd,khd->hgqk', query_rows.astype(jnp.float32), key_rows.astype(jnp.float32)) * scale
        visible = key_pos[None, :] <= query_pos[:, None]
        scores = jnp.where(visible, scores, NEGATIVE)
        peak = lax.optimization_barrier(jnp.max(scores, axis=-1, keepdims=True))
        total = lax.optimization_barrier(jnp.sum(jnp.where(visible, jnp.exp(scores - peak), 0.0), axis=-1, keepdims=True))
        log_total = peak + jnp.log(total)
        weights = jnp.where(visible, jnp.exp(scores - log_total), 0.0).astype(jnp.bfloat16)
        output = jnp.einsum('hgqk,khd->hgqd', weights.astype(jnp.float32), value_rows.astype(jnp.float32))
        return (output.reshape(QUERY_HEAD_COUNT, 2, BLOCK_TOKENS, HEAD_SIZE), log_total.reshape(QUERY_HEAD_COUNT, 2, BLOCK_TOKENS))
    outputs, log_sums = lax.map(one_group, jnp.arange(N_BLK, dtype=jnp.int32))
    outputs = jnp.transpose(outputs, (1, 0, 2, 3, 4)).reshape(QUERY_HEAD_COUNT, SEQUENCE_BLOCKS, BLOCK_TOKENS, HEAD_SIZE)
    log_sums = jnp.transpose(log_sums, (1, 0, 2, 3)).reshape(QUERY_HEAD_COUNT, SEQUENCE_BLOCKS, BLOCK_TOKENS)
    return (outputs, log_sums)
```

```python
import math

import jax
import jax.numpy as jnp
import numpy as np
from jax import lax
from jax.experimental import pallas as pl
from jax.experimental.pallas import tpu as pltpu
from jax.sharding import PartitionSpec as P

MESH = pl.DeviceIdType.MESH
ROPE_BASE = 1000000.0
EPSILON = 1e-06
MASKED = 1e30
BF16 = jnp.bfloat16
F32 = jnp.float32

MODEL = 5120
HEAD = 128
HEADS = 8
BLOCK = 256
SPANS = 64
ROWS = 160
HALF = 80
PART = 256
PARTS = 5
DEPTH = 8 * ROWS


def rope_tables():
    frequency = ROPE_BASE ** (-(np.arange(HEAD // 2, dtype=np.float64) * 2.0 / HEAD))
    frequency = np.concatenate([frequency, frequency])

    def table(positions):
        angles = positions[:, None].astype(np.float64) * frequency[None, :]
        return np.stack([np.cos(angles), np.sin(angles)]).astype(np.float32)

    return table(np.arange(SPANS) * BLOCK), table(np.arange(BLOCK))


def kernel(
    span_pos, tokens, w_query, w_key, w_value, gains, span_table, row_table,
    out, log_sum,
    X, W, kv, q, cosine, sine, scores, staged,
    local_sem, send_sem, recv_sem, out_sem,
):
    blk, head = lax.axis_index("blk"), lax.axis_index("head")
    z, y, c = blk // 8, (blk // 2) % 4, blk % 2
    x, l = head // 2, head % 2
    chip = blk // 2

    def place(z=z, y=y, c=c, x=x, l=l):
        return (z * 8 + y * 2 + c, x * 2 + l)

    zp, zm = place(z=(z + 1) % 4), place(z=(z + 3) % 4)
    yp, ym = place(y=(y + 1) % 4), place(y=(y + 3) % 4)
    xp, xm = place(x=(x + 1) % 4), place(x=(x + 3) % 4)
    lp, sib = place(l=1 - l), place(c=1 - c)
    nxt = (((chip + 1) % 16) * 2 + c, head)
    prv = (((chip + 15) % 16) * 2 + c, head)
    after = (((chip + 2) % 16) * 2, head)
    before = (((chip + 14) % 16) * 2 + 1, head)
    third = jnp.where(c == 0, sib[0], after[0])

    own = [pltpu.make_async_copy(w_key, W.at[0, 0, y, c, :, pl.ds(0, HEAD)], local_sem.at[0]),
           pltpu.make_async_copy(w_value, W.at[0, 0, y, c, :, pl.ds(HEAD, HEAD)], local_sem.at[1])]
    for p in range(1, PARTS):
        own.append(pltpu.make_async_copy(
            w_query.at[:, pl.ds((p - 1) * PART, PART)], W.at[p, 0, y, c], local_sem.at[1 + p]))
    own.append(pltpu.make_async_copy(tokens, X.at[:, x, l], local_sem.at[PARTS + 1]))
    for copy in own:
        copy.start()

    barrier = pltpu.get_barrier_semaphore()
    for device in (zp, zm, yp, ym, xp, xm, lp, sib, prv):
        pl.semaphore_signal(barrier, inc=1, device_id=device, device_id_type=MESH)

    @pl.when(c == 0)
    def _():
        pl.semaphore_signal(barrier, inc=1, device_id=before, device_id_type=MESH)

    pl.semaphore_wait(barrier, 9 + c)
    for copy in own:
        copy.wait()

    started = []

    def send(src, dst, device):
        n = len(started)
        copy = pltpu.make_async_remote_copy(
            src_ref=src, dst_ref=dst, send_sem=send_sem.at[n], recv_sem=recv_sem.at[n],
            device_id=device, device_id_type=MESH)
        copy.start()
        started.append(copy)
        return copy

    A, B = pl.ds(0, HALF), pl.ds(HALF, HALF)
    y_below, y_above = (y + 3) % 4, (y + 1) % 4
    x_below, x_above = (x + 3) % 4, (x + 1) % 4

    def z_send(p, places):
        return (send(W.at[p, 0, places, c], W.at[p, 1, places, c], zp),
                send(W.at[p, 0, places, c], W.at[p, 2, places, c], zm))

    def z_forward(p, places, copies):
        copies[0].wait_recv()
        first = send(W.at[p, 1, places, c, A], W.at[p, 3, places, c, A], zp)
        copies[1].wait_recv()
        return (first, send(W.at[p, 2, places, c, B], W.at[p, 3, places, c, B], zm))

    def y_send(p, slots):
        return (send(W.at[p, slots, y, c], W.at[p, slots, y, c], yp),
                send(W.at[p, slots, y, c], W.at[p, slots, y, c], ym))

    def y_forward(p, slots, copies):
        copies[0].wait_recv()
        first = send(W.at[p, slots, y_below, c, A], W.at[p, slots, y_below, c, A], yp)
        copies[1].wait_recv()
        return (first, send(W.at[p, slots, y_above, c, B], W.at[p, slots, y_above, c, B], ym))

    def x_send(lane):
        return (send(X.at[0, x, lane], X.at[0, x, lane], xp),
                send(X.at[1, x, lane], X.at[1, x, lane], xm),
                send(X.at[1, x, lane], X.at[1, x, lane], xp),
                send(X.at[0, x, lane], X.at[0, x, lane], xm))

    def x_forward(lane, copies):
        copies[0].wait_recv()
        first = send(X.at[0, x_below, lane], X.at[0, x_below, lane], xp)
        copies[1].wait_recv()
        return (first, send(X.at[1, x_above, lane], X.at[1, x_above, lane], xm))

    def core_send(p):
        return send(W.at[p, :, :, c], W.at[p, :, :, c], sib)

    def arrive(*copies):
        for copy in copies:
            copy.wait_recv()

    first_slot, other_slots, all_slots = pl.ds(0, 1), pl.ds(1, 3), pl.ds(0, 4)
    every_y = pl.ds(0, 4)

    def tables():
        for s in range(2):
            chosen = lax.broadcasted_iota(jnp.int32, (SPANS, HEAD), 0) == span_pos[blk * 2 + s]
            span_cos = jnp.sum(jnp.where(chosen, span_table[0], 0.0), axis=0, keepdims=True)
            span_sin = jnp.sum(jnp.where(chosen, span_table[1], 0.0), axis=0, keepdims=True)
            cosine[s] = (span_cos * row_table[0] - span_sin * row_table[1]).reshape(4, 2, 32, HEAD)
            whole = span_sin * row_table[0] + span_cos * row_table[1]
            lane = lax.broadcasted_iota(jnp.int32, (BLOCK, HEAD), 1)
            sine[s] = jnp.where(lane < HEAD // 2, -whole, whole).reshape(4, 2, 32, HEAD)

    def project(p, lane):
        total = None
        for slot, place_z in enumerate((z, (z + 3) % 4, (z + 1) % 4, (z + 2) % 4)):
            depth = pl.ds(pl.multiple_of(place_z * DEPTH, DEPTH), DEPTH)
            rows = X[:, :, pl.ds(lane, 1), :, depth].reshape(BLOCK, DEPTH)
            term = jnp.dot(rows, W[p, slot].reshape(DEPTH, PART), preferred_element_type=F32)
            total = term if total is None else total + term
        return total

    def norm_rotate(raw, gain, lane):
        mean_sq = jnp.mean(raw * raw, axis=-1, keepdims=True)
        normed = raw * lax.rsqrt(mean_sq + EPSILON) * gain
        cos_rows = cosine[:, :, pl.ds(lane, 1)].reshape(BLOCK, HEAD)
        sin_rows = sine[:, :, pl.ds(lane, 1)].reshape(BLOCK, HEAD)
        turned = normed * cos_rows + pltpu.roll(normed, HEAD // 2, 1) * sin_rows
        return turned.astype(BF16).reshape(2, 4, 1, 32, HEAD)

    def keys_values(lane):
        raw = project(0, lane)
        kv[0, :, :, pl.ds(lane, 1), :, pl.ds(0, HEAD)] = norm_rotate(raw[:, :HEAD], gains[1:2], lane)
        kv[0, :, :, pl.ds(lane, 1), :, pl.ds(HEAD, HEAD)] = (
            raw[:, HEAD:].astype(BF16).reshape(2, 4, 1, 32, HEAD))

    def queries(p, lane):
        raw = project(p, lane)
        for j in range(2):
            q[2 * (p - 1) + j, :, :, pl.ds(lane, 1)] = norm_rotate(
                raw[:, j * HEAD:(j + 1) * HEAD], gains[0:1], lane)

    def kv_send(lane):
        ahead = send(kv.at[0, :, :, lane], kv.at[2, :, :, lane], nxt)
        slot = jnp.where(c == 0, 1, 3)
        return ahead, send(kv.at[0, :, :, lane], kv.at[slot, :, :, lane], (third, head))

    def kv_forward(lane, ahead):
        arrive(ahead)
        slot = jnp.where(c == 0, 3, 1)
        return send(kv.at[2, :, :, lane], kv.at[slot, :, :, lane], sib)

    z0 = z_send(0, y)
    y4 = y_send(4, first_slot)
    y0 = y_send(0, first_slot)
    x_own = x_send(l)
    x_lane = send(X.at[:, x, l], X.at[:, x, l], lp)
    z1 = z_send(1, y)
    tables()
    z0f = z_forward(0, y, z0)
    y4f = y_forward(4, first_slot, y4)
    y0f = y_forward(0, first_slot, y0)
    arrive(*z0f)
    y0r = y_send(0, other_slots)
    z1f = z_forward(1, y, z1)
    z2 = z_send(2, y)
    x_ownf = x_forward(l, x_own)
    arrive(x_lane)
    x_oth = x_send(1 - l)
    arrive(*z1f)
    y1 = y_send(1, all_slots)
    y0rf = y_forward(0, other_slots, y0r)
    z2f = z_forward(2, y, z2)
    z3 = z_send(3, y)
    arrive(*y0f, *y0rf)
    c0 = core_send(0)
    arrive(*z2f)
    y2 = y_send(2, all_slots)
    arrive(x_own[2], x_own[3], *x_ownf)
    arrive(c0)
    keys_values(l)
    kv_a, kv_a3 = kv_send(l)
    y1f = y_forward(1, all_slots, y1)
    z3f = z_forward(3, y, z3)
    arrive(*y4f)
    z4 = z_send(4, every_y)
    arrive(*z3f)
    y3 = y_send(3, all_slots)
    x_othf = x_forward(1 - l, x_oth)
    arrive(*y1f)
    c1 = core_send(1)
    kv_af = kv_forward(l, kv_a)
    y2f = y_forward(2, all_slots, y2)
    arrive(c1)
    queries(1, l)
    z4f = z_forward(4, every_y, z4)
    arrive(*y2f)
    c2 = core_send(2)
    arrive(x_oth[2], x_oth[3], *x_othf)
    keys_values(1 - l)
    kv_b, kv_b3 = kv_send(1 - l)
    y3f = y_forward(3, all_slots, y3)
    queries(1, 1 - l)
    arrive(c2)
    queries(2, l)
    kv_bf = kv_forward(1 - l, kv_b)
    queries(2, 1 - l)
    arrive(*z4f)
    c4 = core_send(4)
    arrive(*y3f)
    c3 = core_send(3)
    arrive(c4)
    queries(4, l)
    queries(4, 1 - l)
    arrive(c3)
    queries(3, l)
    queries(3, 1 - l)
    arrive(kv_a3, kv_af, kv_b3, kv_bf)

    own_pos = [span_pos[blk * 2 + s] for s in range(2)]
    offsets = []
    for step in range(4):
        source = (blk + 32 - step) % 32
        for s in range(2):
            pos = span_pos[source * 2 + s]
            offsets.append([jnp.where(pos <= own_pos[i], 0.0, MASKED).astype(F32) for i in range(2)])
    factor = HEAD ** (-0.5) * math.log2(math.e)
    causal = (lax.broadcasted_iota(jnp.int32, (BLOCK, BLOCK), 0)
              >= lax.broadcasted_iota(jnp.int32, (BLOCK, BLOCK), 1))

    def attend(h, carry):
        rows = q[h].reshape(2 * BLOCK, HEAD)
        peaks = [None, None]
        for tile in range(8):
            keys = kv[tile // 2, tile % 2, :, :, :, pl.ds(0, HEAD)].reshape(BLOCK, HEAD)
            found = lax.dot_general(rows, keys, (((1,), (1,)), ((), ())), preferred_element_type=F32) * factor
            for i in range(2):
                part = found[i * BLOCK:(i + 1) * BLOCK]
                if tile == i:
                    part = jnp.where(causal, part, -MASKED)
                scores[i, :, pl.ds(tile * BLOCK, BLOCK)] = part
                peak = jnp.maximum(part[:, :HEAD], part[:, HEAD:]) - offsets[tile][i]
                peaks[i] = peak if peaks[i] is None else jnp.maximum(peaks[i], peak)
        for i in range(2):
            peak = jnp.max(peaks[i], axis=-1, keepdims=True)
            total = jnp.zeros((BLOCK, HEAD), F32)
            summed = jnp.zeros((BLOCK, HEAD), F32)
            for tile in range(8):
                weights = jnp.exp2(scores[i, :, pl.ds(tile * BLOCK, BLOCK)] - (peak + offsets[tile][i]))
                total = total + (weights[:, :HEAD] + weights[:, HEAD:])
                values = kv[tile // 2, tile % 2, :, :, :, pl.ds(HEAD, HEAD)].reshape(BLOCK, HEAD)
                summed = summed + jnp.dot(weights.astype(BF16), values, preferred_element_type=F32)
            whole = jnp.sum(total, axis=-1, keepdims=True)
            staged[h, i] = summed / whole
            lse = peak * math.log(2.0) + jnp.log(whole)
            log_sum[h, pl.ds(i, 1), :] = jnp.transpose(jnp.broadcast_to(lse, (BLOCK, HEAD)))[0:1, :]
        pltpu.make_async_copy(staged.at[h], out.at[h], out_sem.at[h]).start()
        return carry

    lax.fori_loop(0, HEADS, attend, 0)

    def finish(h, carry):
        pltpu.make_async_copy(staged.at[h], out.at[h], out_sem.at[h]).wait()
        return carry

    lax.fori_loop(0, HEADS, finish, 0)
    for copy in started:
        copy.wait_send()


SENDS = 68


def shards(tokens, span_pos, w_query, key_projection, value_projection, query_gain, key_gain):
    span_table, row_table = rope_tables()
    gains = jnp.stack([query_gain, key_gain])
    vmem, anywhere = pl.BlockSpec(memory_space=pltpu.VMEM), pl.BlockSpec(memory_space=pl.ANY)
    return pl.pallas_call(
        kernel,
        out_shape=(
            jax.ShapeDtypeStruct((HEADS, 2, BLOCK, HEAD), F32),
            jax.ShapeDtypeStruct((HEADS, 2, BLOCK), F32),
        ),
        in_specs=[pl.BlockSpec(memory_space=pltpu.SMEM), anywhere, anywhere, anywhere, anywhere, vmem, vmem, vmem],
        out_specs=(anywhere, vmem),
        scratch_shapes=[
            pltpu.VMEM((2, 4, 2, 32, MODEL), BF16),
            pltpu.VMEM((PARTS, 4, 4, 2, ROWS, PART), BF16),
            pltpu.VMEM((4, 2, 4, 2, 32, 2 * HEAD), BF16),
            pltpu.VMEM((HEADS, 2, 4, 2, 32, HEAD), BF16),
            pltpu.VMEM((2, 4, 2, 32, HEAD), F32),
            pltpu.VMEM((2, 4, 2, 32, HEAD), F32),
            pltpu.VMEM((2, BLOCK, 8 * BLOCK), F32),
            pltpu.VMEM((HEADS, 2, BLOCK, HEAD), F32),
            pltpu.SemaphoreType.DMA((PARTS + 2,)),
            pltpu.SemaphoreType.DMA((SENDS,)),
            pltpu.SemaphoreType.DMA((SENDS,)),
            pltpu.SemaphoreType.DMA((HEADS,)),
        ],
        compiler_params=pltpu.CompilerParams(
            collective_id=0, has_side_effects=True, vmem_limit_bytes=56 * 2**20),
        name="layer",
    )(span_pos, tokens, w_query, key_projection, value_projection, gains, span_table, row_table)


def solution(mesh):
    placed = (
        P("blk", "head", None),
        P(),
        P("blk", "head"),
        P("blk", "head"),
        P("blk", "head"),
        P(),
        P(),
    )
    return jax.shard_map(
        shards,
        mesh=mesh,
        in_specs=placed,
        out_specs=(P("head", "blk", None, None), P("head", "blk", None)),
        check_vma=False,
    )
```

```python
import math

import jax
import jax.numpy as jnp
import numpy as np
from jax import lax
from jax.experimental import pallas as pl
from jax.experimental.pallas import tpu as pltpu
from jax.sharding import PartitionSpec as P

MESH = pl.DeviceIdType.MESH
ROPE_BASE = 1000000.0
EPSILON = 1e-06
MASKED = 1e30
LEAST = -1e28
BF16 = jnp.bfloat16
F32 = jnp.float32

MODEL = 5120
HEAD = 128
HEADS = 8
BLOCK = 256
SPANS = 64
ROWS = 160
HALF = 80
SPLIT = 64
PART = 256
PARTS = 5
DEPTH = 8 * ROWS


def rope_tables():
    frequency = ROPE_BASE ** (-(np.arange(HEAD // 2, dtype=np.float64) * 2.0 / HEAD))
    frequency = np.concatenate([frequency, frequency])

    def table(positions):
        angles = positions[:, None].astype(np.float64) * frequency[None, :]
        return np.stack([np.cos(angles), np.sin(angles)]).astype(np.float32)

    return table(np.arange(SPANS) * BLOCK), table(np.arange(BLOCK))


def kernel(
    span_pos, tokens, w_query, w_key, w_value, query_gain, key_gain, span_table, row_table,
    out, log_sum,
    X, W, kv, q, cosine, sine, masking, summing, causal, partial, peaks, staged,
    local_sem, send_sem, recv_sem, out_sem,
):
    blk, head = lax.axis_index("blk"), lax.axis_index("head")
    z, y, c = blk // 8, (blk // 2) % 4, blk % 2
    x, l = head // 2, head % 2
    chip = blk // 2

    def place(z=z, y=y, c=c, x=x, l=l):
        return (z * 8 + y * 2 + c, x * 2 + l)

    zp, zm = place(z=(z + 1) % 4), place(z=(z + 3) % 4)
    yp, ym = place(y=(y + 1) % 4), place(y=(y + 3) % 4)
    xp, xm = place(x=(x + 1) % 4), place(x=(x + 3) % 4)
    lp, sib = place(l=1 - l), place(c=1 - c)
    nxt = (((chip + 1) % 16) * 2 + c, head)
    prv = (((chip + 15) % 16) * 2 + c, head)
    after = (((chip + 2) % 16) * 2, head)
    before = (((chip + 14) % 16) * 2 + 1, head)
    third = jnp.where(c == 0, sib[0], after[0])

    own = [pltpu.make_async_copy(w_key, W.at[0, 0, y, c, :, pl.ds(0, HEAD)], local_sem.at[0]),
           pltpu.make_async_copy(w_value, W.at[0, 0, y, c, :, pl.ds(HEAD, HEAD)], local_sem.at[1])]
    for p in range(1, PARTS):
        own.append(pltpu.make_async_copy(
            w_query.at[:, pl.ds((p - 1) * PART, PART)], W.at[p, 0, y, c], local_sem.at[1 + p]))
    own.append(pltpu.make_async_copy(tokens, X.at[:, x, l], local_sem.at[PARTS + 1]))
    for copy in own:
        copy.start()

    barrier = pltpu.get_barrier_semaphore()
    for device in (zp, zm, yp, ym, xp, xm, lp, sib, prv):
        pl.semaphore_signal(barrier, inc=1, device_id=device, device_id_type=MESH)

    @pl.when(c == 0)
    def _():
        pl.semaphore_signal(barrier, inc=1, device_id=before, device_id_type=MESH)

    pl.semaphore_wait(barrier, 9 + c)
    for copy in own:
        copy.wait()

    started = []

    def send(src, dst, device):
        n = len(started)
        copy = pltpu.make_async_remote_copy(
            src_ref=src, dst_ref=dst, send_sem=send_sem.at[n], recv_sem=recv_sem.at[n],
            device_id=device, device_id_type=MESH)
        copy.start()
        started.append(copy)
        return copy

    A, B = pl.ds(0, HALF), pl.ds(HALF, HALF)
    low, high = pl.ds(0, SPLIT), pl.ds(SPLIT, ROWS - SPLIT)
    y_below, y_above = (y + 3) % 4, (y + 1) % 4
    x_below, x_above = (x + 3) % 4, (x + 1) % 4
    all_rows, all_cols = pl.ds(0, ROWS), pl.ds(0, PART)
    left, right = pl.ds(0, HEAD), pl.ds(HEAD, HEAD)
    every_y, early, near, far, parts = pl.ds(0, 4), pl.ds(0, 3), pl.ds(1, 2), 3, pl.ds(0, PARTS)

    def z_up(p, places=y, cols=all_cols):
        return send(W.at[p, 0, places, c, all_rows, cols], W.at[p, 1, places, c, all_rows, cols], zp)

    def z_down(p, places=y, cols=all_cols):
        return send(W.at[p, 0, places, c, all_rows, cols], W.at[p, 2, places, c, all_rows, cols], zm)

    def z_on_up(p, places=y, cols=all_cols):
        return send(W.at[p, 1, places, c, A, cols], W.at[p, 3, places, c, A, cols], zp)

    def z_on_down(p, places=y, cols=all_cols):
        return send(W.at[p, 2, places, c, B, cols], W.at[p, 3, places, c, B, cols], zm)

    def y_send(device, p, slots, cols=all_cols):
        block = W.at[p, slots, y, c, all_rows, cols]
        return send(block, block, device)

    def y_on_up(p, slots, cols=all_cols):
        block = W.at[p, slots, y_below, c, low, cols]
        return send(block, block, yp)

    def y_on_down(p, slots, cols=all_cols):
        block = W.at[p, slots, y_above, c, high, cols]
        return send(block, block, ym)

    def x_send(lane, span, device):
        block = X.at[span, x, lane]
        return send(block, block, device)

    def x_on_up(lane):
        block = X.at[0, x_below, lane]
        return send(block, block, xp)

    def x_on_down(lane):
        block = X.at[1, x_above, lane]
        return send(block, block, xm)

    def core_send(p, slots=pl.ds(0, 4), cols=all_cols):
        block = W.at[p, slots, :, c, :, cols]
        return send(block, block, sib)

    def arrive(*copies):
        for copy in copies:
            copy.wait_recv()

    def tables():
        for s in range(2):
            chosen = lax.broadcasted_iota(jnp.int32, (SPANS, HEAD), 0) == span_pos[blk * 2 + s]
            span_cos = jnp.sum(jnp.where(chosen, span_table[0], 0.0), axis=0, keepdims=True)
            span_sin = jnp.sum(jnp.where(chosen, span_table[1], 0.0), axis=0, keepdims=True)
            cosine[s] = (span_cos * row_table[0] - span_sin * row_table[1]).reshape(4, 2, 32, HEAD)
            whole = span_sin * row_table[0] + span_cos * row_table[1]
            lane = lax.broadcasted_iota(jnp.int32, (BLOCK, HEAD), 1)
            sine[s] = jnp.where(lane < HEAD // 2, -whole, whole).reshape(4, 2, 32, HEAD)
        lane = lax.broadcasted_iota(jnp.int32, (HEADS, 2, 4, 2, 32, HEAD), 5)
        span = lax.broadcasted_iota(jnp.int32, (HEADS, 2, 4, 2, 32, HEAD), 1)
        q[:, :, :, :, :, pl.ds(HEAD, HEAD)] = jnp.where(lane == span, 1.0, 0.0).astype(BF16)
        for part in range(2):
            summing[part, :, pl.ds(HEAD, HEAD)] = jnp.ones((4 * BLOCK, HEAD), BF16)

    def project(p, lane):
        total = None
        for slot, place_z in enumerate((z, (z + 3) % 4, (z + 1) % 4, (z + 2) % 4)):
            depth = pl.ds(pl.multiple_of(place_z * DEPTH, DEPTH), DEPTH)
            rows = X[:, :, pl.ds(lane, 1), :, depth].reshape(BLOCK, DEPTH)
            term = jnp.dot(rows, W[p, slot].reshape(DEPTH, PART), preferred_element_type=F32)
            total = term if total is None else total + term
        return total

    def norm_rotate(raw, gain, lane):
        mean_sq = jnp.mean(raw * raw, axis=-1, keepdims=True)
        normed = raw * lax.rsqrt(mean_sq + EPSILON) * gain
        cos_rows = cosine[:, :, pl.ds(lane, 1)].reshape(BLOCK, HEAD)
        sin_rows = sine[:, :, pl.ds(lane, 1)].reshape(BLOCK, HEAD)
        turned = normed * cos_rows + pltpu.roll(normed, HEAD // 2, 1) * sin_rows
        return turned.astype(BF16).reshape(2, 4, 1, 32, HEAD)

    def keys_values(lane):
        raw = project(0, lane)
        kv[0, :, :, pl.ds(lane, 1), :, pl.ds(0, HEAD)] = norm_rotate(raw[:, :HEAD], key_gain[...], lane)
        kv[0, :, :, pl.ds(lane, 1), :, pl.ds(HEAD, HEAD)] = (
            raw[:, HEAD:].astype(BF16).reshape(2, 4, 1, 32, HEAD))

    def queries(p, lane):
        raw = project(p, lane)
        for j in range(2):
            q[2 * (p - 1) + j, :, :, pl.ds(lane, 1), :, pl.ds(0, HEAD)] = norm_rotate(
                raw[:, j * HEAD:(j + 1) * HEAD], query_gain[...], lane)

    def kv_ahead(lane):
        return send(kv.at[0, :, :, lane], kv.at[2, :, :, lane], nxt)

    def kv_third(lane):
        slot = jnp.where(c == 0, 1, 3)
        return send(kv.at[0, :, :, lane], kv.at[slot, :, :, lane], (third, head))

    def kv_across(lane):
        slot = jnp.where(c == 0, 3, 1)
        return send(kv.at[2, :, :, lane], kv.at[slot, :, :, lane], sib)

    own_pos = [span_pos[blk * 2 + s] for s in range(2)]

    def gather_keys(lane, part):
        column = lax.broadcasted_iota(jnp.int32, (HEAD, HEAD), 1)
        for step in range(4):
            source = (blk + 32 - step) % 32
            block = kv[step, :, :, pl.ds(lane, 1)].reshape(BLOCK, 2 * HEAD)
            rows = pl.ds(step * BLOCK, BLOCK)
            masking[part, rows, pl.ds(0, HEAD)] = block[:, :HEAD]
            summing[part, rows, pl.ds(0, HEAD)] = block[:, HEAD:]
            for s in range(2):
                pos = span_pos[source * 2 + s]
                hide = [jnp.where(pos <= own_pos[i], 0.0, -MASKED).astype(F32) for i in range(2)]
                masking[part, pl.ds(step * BLOCK + s * HEAD, HEAD), pl.ds(HEAD, HEAD)] = jnp.where(
                    column == 0, hide[0], jnp.where(column == 1, hide[1], 0.0)).astype(BF16)
        key = lax.broadcasted_iota(jnp.int32, (BLOCK, HEAD), 1)
        place_in = key // 32 * 64 + lane * 32 + key % 32
        hidden = jnp.where(lax.broadcasted_iota(jnp.int32, (BLOCK, HEAD), 0) >= place_in, 0.0, -MASKED)
        for i in range(2):
            causal[part, pl.ds(i * BLOCK, BLOCK), pl.ds(i * HEAD, HEAD)] = hidden
            causal[part, pl.ds(i * BLOCK, BLOCK), pl.ds((1 - i) * HEAD, HEAD)] = jnp.zeros((BLOCK, HEAD), F32)

    factor = HEAD ** (-0.5) * math.log2(math.e)

    def attend(p, half):
        first = half == 0
        for h in (2 * p - 2, 2 * p - 1):
            rows = q[h].reshape(2 * BLOCK, 2 * HEAD)
            peak = None
            found = []
            for step in range(4):
                keys = masking[half, pl.ds(step * BLOCK, BLOCK), :]
                part = lax.dot_general(rows, keys, (((1,), (1,)), ((), ())), preferred_element_type=F32) * factor
                if step == 0:
                    part = part + causal[half]
                found.append(part)
                top = jnp.maximum(part[:, :HEAD], part[:, HEAD:])
                peak = top if peak is None else jnp.maximum(peak, top)
            peak = jnp.max(peak, axis=-1, keepdims=True)
            if first:
                peak = jnp.maximum(peak, LEAST)
            else:
                before_peak = peaks[h][:, 0:1]
                peak = jnp.maximum(peak, before_peak)
            weights = jnp.concatenate([jnp.exp2(part - peak).astype(BF16) for part in found], axis=1)
            summed = jnp.dot(weights, summing[half], preferred_element_type=F32)
            if first:
                partial[h] = summed
                peaks[h] = jnp.broadcast_to(peak, (2 * BLOCK, HEAD))
            else:
                summed = summed + partial[h] * jnp.exp2(before_peak - peak)
                whole = summed[:, HEAD:]
                staged[h] = (summed[:, :HEAD] / whole).reshape(2, BLOCK, HEAD)
                lse = jnp.transpose(peak * math.log(2.0) + jnp.log(whole))
                for i in range(2):
                    log_sum[h, pl.ds(i, 1), :] = lse[0:1, i * BLOCK:(i + 1) * BLOCK]
                pltpu.make_async_copy(staged.at[h], out.at[h], out_sem.at[h]).start()

    z0_p = z_up(0)
    ya_m = y_send(ym, parts, 0)
    z0_m = z_down(0)
    z1_m = z_down(1)
    z1_p = z_up(1)
    lane_b = x_send(l, 1, lp)
    xo_a_p = x_send(l, 0, xp)
    xo_b_m = x_send(l, 1, xm)
    ya_p = y_send(yp, parts, 0)
    arrive(z0_p)
    z0_fp = z_on_up(0)
    arrive(z0_m)
    y0_m = y_send(ym, 0, near)
    xo_a_m = x_send(l, 0, xm)
    xo_b_p = x_send(l, 1, xp)
    z0_fm = z_on_down(0)
    arrive(z1_p, z1_m)
    y1_m = y_send(ym, 1, near)
    y0_p = y_send(yp, 0, near)
    arrive(ya_m)
    ya_fm = y_on_down(parts, 0)
    z1_fp = z_on_up(1)
    arrive(ya_p)
    ya_fp = y_on_up(parts, 0)
    tables()
    arrive(y0_m)
    y0_fm = y_on_down(0, near)
    z2_m = z_down(2)
    z2_p = z_up(2)
    arrive(lane_b)
    xt_b_p = x_send(1 - l, 1, xp)
    z1_fm = z_on_down(1)
    arrive(xo_a_p)
    xo_fa = x_on_up(l)
    lane_a = x_send(l, 0, lp)
    y1_p = y_send(yp, 1, near)
    arrive(y0_p)
    y0_fp = y_on_up(0, near)
    arrive(y1_m)
    y1_fm = y_on_down(1, near)
    xt_b_m = x_send(1 - l, 1, xm)
    arrive(z0_fp, z0_fm)
    y0s_p = y_send(yp, 0, far)
    arrive(y1_p)
    y1_fp = y_on_up(1, near)
    arrive(z1_fp, z1_fm)
    y1s_p = y_send(yp, 1, far)
    y0s_m = y_send(ym, 0, far)
    y1s_m = y_send(ym, 1, far)
    arrive(z2_m)
    z2_fm = z_on_down(2)
    arrive(z2_p)
    z2_fp = z_on_up(2)
    y2_m = y_send(ym, 2, near)
    arrive(xo_b_m)
    xo_fb = x_on_down(l)
    arrive(y0_fp, y0_fm, ya_fp, ya_fm)
    c0n = core_send(0, early)
    arrive(y0s_p)
    y0s_fp = y_on_up(0, far)
    y2_p = y_send(yp, 2, near)
    arrive(y1_fp, y1_fm)
    c1n = core_send(1, early)
    z3_p = z_up(3)
    arrive(y0s_m)
    y0s_fm = y_on_down(0, far)
    z3_m = z_down(3)
    arrive(lane_a)
    xt_a_p = x_send(1 - l, 0, xp)
    zL_p = z_up(4, cols=left)
    xt_a_m = x_send(1 - l, 0, xm)
    arrive(y1s_p)
    y1s_fp = y_on_up(1, far)
    zL_m = z_down(4, cols=left)
    arrive(y1s_m)
    y1s_fm = y_on_down(1, far)
    arrive(z2_fp, z2_fm)
    y2s_p = y_send(yp, 2, far)
    arrive(y2_m)
    y2_fm = y_on_down(2, near)
    y2s_m = y_send(ym, 2, far)
    arrive(y2_p)
    y2_fp = y_on_up(2, near)
    zR_p = z_up(4, every_y, right)
    zR_m = z_down(4, every_y, right)
    arrive(y0s_fp, y0s_fm)
    c0f = core_send(0, far)
    arrive(z3_p, z3_m)
    y3_p = y_send(yp, 3, near)
    arrive(y1s_fp, y1s_fm)
    c1f = core_send(1, far)
    arrive(xt_b_m)
    xt_fb = x_on_down(1 - l)
    y3_m = y_send(ym, 3, near)
    z3_fp = z_on_up(3)
    arrive(zL_p, zL_m)
    yL_m = y_send(ym, 4, near, cols=left)
    arrive(c0n, c0f, xo_b_p, xo_a_m, xo_fa, xo_fb)
    keys_values(l)
    arrive(xt_a_p)
    xt_fa = x_on_up(1 - l)
    knA = kv_ahead(l)
    yL_p = y_send(yp, 4, near, cols=left)
    z3_fm = z_on_down(3)
    arrive(y2s_m)
    y2s_fm = y_on_down(2, far)
    arrive(y2s_p)
    y2s_fp = y_on_up(2, far)
    zL_fm = z_on_down(4, cols=left)
    zL_fp = z_on_up(4, cols=left)
    arrive(y3_p)
    y3_fp = y_on_up(3, near)
    arrive(y2_fp, y2_fm)
    c2n = core_send(2, early)
    arrive(y3_m)
    y3_fm = y_on_down(3, near)
    arrive(zR_p)
    zR_fp = z_on_up(4, every_y, right)
    arrive(zR_m)
    zR_fm = z_on_down(4, every_y, right)
    arrive(c1n, c1f)
    queries(1, l)
    k3A = kv_third(l)
    arrive(z3_fp, z3_fm)
    y3s_p = y_send(yp, 3, far)
    y3s_m = y_send(ym, 3, far)
    arrive(knA)
    kfA = kv_across(l)
    arrive(yL_p)
    yL_fp = y_on_up(4, near, cols=left)
    arrive(yL_m)
    yL_fm = y_on_down(4, near, cols=left)
    arrive(y2s_fp, y2s_fm)
    c2f = core_send(2, far)
    arrive(zL_fp, zL_fm)
    yLs_p = y_send(yp, 4, far, cols=left)
    yLs_m = y_send(ym, 4, far, cols=left)
    arrive(xt_b_p, xt_a_m, xt_fa, xt_fb)
    keys_values(1 - l)
    k3B = kv_third(1 - l)
    knB = kv_ahead(1 - l)
    queries(1, 1 - l)
    arrive(k3A, kfA)
    gather_keys(l, 0)
    attend(1, 0)
    arrive(y3_fp, y3_fm)
    c3n = core_send(3, early)
    arrive(y3s_m)
    y3s_fm = y_on_down(3, far)
    arrive(y3s_p)
    y3s_fp = y_on_up(3, far)
    arrive(zR_fp, zR_fm)
    c4b = core_send(4, cols=right)
    arrive(yLs_p)
    yLs_fp = y_on_up(4, far, cols=left)
    arrive(c2n, c2f)
    queries(2, 1 - l)
    arrive(yLs_m)
    yLs_fm = y_on_down(4, far, cols=left)
    queries(2, l)
    arrive(knB)
    kfB = kv_across(1 - l)
    attend(2, 0)
    arrive(y3s_fp, y3s_fm)
    c3f = core_send(3, far)
    arrive(yL_fp, yL_fm, yLs_fp, yLs_fm)
    c4a = core_send(4, cols=left)
    arrive(k3B, kfB)
    gather_keys(1 - l, 1)
    attend(2, 1)
    attend(1, 1)
    arrive(c3n, c3f)
    queries(3, 1 - l)
    queries(3, l)
    arrive(c4a, c4b)
    queries(4, 1 - l)
    attend(3, 0)
    queries(4, l)
    attend(3, 1)
    attend(4, 0)
    attend(4, 1)

    def finish(h, carry):
        pltpu.make_async_copy(staged.at[h], out.at[h], out_sem.at[h]).wait()
        return carry

    lax.fori_loop(0, HEADS, finish, 0)
    for copy in started:
        copy.wait_send()


SENDS = 98


def shards(tokens, span_pos, w_query, key_projection, value_projection, query_gain, key_gain):
    span_table, row_table = rope_tables()
    vmem, anywhere = pl.BlockSpec(memory_space=pltpu.VMEM), pl.BlockSpec(memory_space=pl.ANY)
    hbm = pl.BlockSpec(memory_space=pltpu.HBM)
    return pl.pallas_call(
        kernel,
        out_shape=(
            jax.ShapeDtypeStruct((HEADS, 2, BLOCK, HEAD), F32),
            jax.ShapeDtypeStruct((HEADS, 2, BLOCK), F32),
        ),
        in_specs=[pl.BlockSpec(memory_space=pltpu.SMEM), hbm, hbm, hbm, hbm, vmem, vmem, vmem, vmem],
        out_specs=(anywhere, vmem),
        scratch_shapes=[
            pltpu.VMEM((2, 4, 2, 32, MODEL), BF16),
            pltpu.VMEM((PARTS, 4, 4, 2, ROWS, PART), BF16),
            pltpu.VMEM((4, 2, 4, 2, 32, 2 * HEAD), BF16),
            pltpu.VMEM((HEADS, 2, 4, 2, 32, 2 * HEAD), BF16),
            pltpu.VMEM((2, 4, 2, 32, HEAD), F32),
            pltpu.VMEM((2, 4, 2, 32, HEAD), F32),
            pltpu.VMEM((2, 4 * BLOCK, 2 * HEAD), BF16),
            pltpu.VMEM((2, 4 * BLOCK, 2 * HEAD), BF16),
            pltpu.VMEM((2, 2 * BLOCK, 2 * HEAD), F32),
            pltpu.VMEM((HEADS, 2 * BLOCK, 2 * HEAD), F32),
            pltpu.VMEM((HEADS, 2 * BLOCK, HEAD), F32),
            pltpu.VMEM((HEADS, 2, BLOCK, HEAD), F32),
            pltpu.SemaphoreType.DMA((PARTS + 2,)),
            pltpu.SemaphoreType.DMA((SENDS,)),
            pltpu.SemaphoreType.DMA((SENDS,)),
            pltpu.SemaphoreType.DMA((HEADS,)),
        ],
        compiler_params=pltpu.CompilerParams(
            collective_id=0, has_side_effects=True, vmem_limit_bytes=56 * 2**20),
        name="layer",
    )(span_pos, tokens, w_query, key_projection, value_projection, query_gain[None], key_gain[None],
      span_table, row_table)


def solution(mesh):
    placed = (
        P("blk", "head", None),
        P(),
        P("blk", "head"),
        P("blk", "head"),
        P("blk", "head"),
        P(),
        P(),
    )
    return jax.shard_map(
        shards,
        mesh=mesh,
        in_specs=placed,
        out_specs=(P("head", "blk", None, None), P("head", "blk", None)),
        check_vma=False,
    )
```

```python
import math

import jax
import jax.numpy as jnp
import numpy as np
from jax import lax
from jax.experimental import pallas as pl
from jax.experimental.pallas import tpu as pltpu
from jax.sharding import PartitionSpec as P

MESH = pl.DeviceIdType.MESH
ROPE_BASE = 1000000.0
EPSILON = 1e-06
MASKED = 1e30
LEAST = -1e28
BF16 = jnp.bfloat16
F32 = jnp.float32

MODEL = 5120
HEAD = 128
HEADS = 8
BLOCK = 256
SPANS = 64
ROWS = 160
HALF = 80
SPLIT = 64
PART = 256
PARTS = 5
DEPTH = 8 * ROWS


def rope_tables():
    frequency = ROPE_BASE ** (-(np.arange(HEAD // 2, dtype=np.float64) * 2.0 / HEAD))
    frequency = np.concatenate([frequency, frequency])

    def table(positions):
        angles = positions[:, None].astype(np.float64) * frequency[None, :]
        return np.stack([np.cos(angles), np.sin(angles)]).astype(np.float32)

    return table(np.arange(SPANS) * BLOCK), table(np.arange(BLOCK))


def kernel(
    span_pos, tokens, w_query, w_key, w_value, query_gain, key_gain, span_table, row_table,
    out, log_sum,
    X, W, kv, q, cosine, sine, masking, summing, causal, partial, peaks, staged,
    local_sem, send_sem, recv_sem, out_sem,
):
    blk, head = lax.axis_index("blk"), lax.axis_index("head")
    z, y, c = blk // 8, (blk // 2) % 4, blk % 2
    x, l = head // 2, head % 2
    chip = blk // 2

    def place(z=z, y=y, c=c, x=x, l=l):
        return (z * 8 + y * 2 + c, x * 2 + l)

    z_up_at, z_down_at = (z + 1 + 2 * l) % 4, (z + 3 + 2 * l) % 4
    zp, zm = place(z=z_up_at), place(z=z_down_at)
    yp, ym = place(y=(y + 1) % 4), place(y=(y + 3) % 4)
    xp, xm = place(x=(x + 1) % 4), place(x=(x + 3) % 4)
    lp, sib = place(l=1 - l), place(c=1 - c)
    nxt = (((chip + 1) % 16) * 2 + c, head)
    prv = (((chip + 15) % 16) * 2 + c, head)
    after = (((chip + 2) % 16) * 2, head)
    before = (((chip + 14) % 16) * 2 + 1, head)
    third = jnp.where(c == 0, sib[0], after[0])

    own = [pltpu.make_async_copy(w_key, W.at[0, 0, y, c, :, pl.ds(0, HEAD)], local_sem.at[0]),
           pltpu.make_async_copy(w_value, W.at[0, 0, y, c, :, pl.ds(HEAD, HEAD)], local_sem.at[1])]
    for p in range(1, PARTS):
        own.append(pltpu.make_async_copy(
            w_query.at[:, pl.ds((p - 1) * PART, PART)], W.at[p, 0, y, c], local_sem.at[1 + p]))
    own.append(pltpu.make_async_copy(tokens, X.at[:, x, l], local_sem.at[PARTS + 1]))
    for copy in own:
        copy.start()

    barrier = pltpu.get_barrier_semaphore()
    for device in (zp, zm, yp, ym, xp, xm, lp, sib, prv):
        pl.semaphore_signal(barrier, inc=1, device_id=device, device_id_type=MESH)

    @pl.when(c == 0)
    def _():
        pl.semaphore_signal(barrier, inc=1, device_id=before, device_id_type=MESH)

    pl.semaphore_wait(barrier, 9 + c)
    for copy in own:
        copy.wait()

    started = []

    def send(src, dst, device):
        n = len(started)
        copy = pltpu.make_async_remote_copy(
            src_ref=src, dst_ref=dst, send_sem=send_sem.at[n], recv_sem=recv_sem.at[n],
            device_id=device, device_id_type=MESH)
        copy.start()
        started.append(copy)
        return copy

    A, B = pl.ds(0, HALF), pl.ds(HALF, HALF)
    low, high = pl.ds(0, SPLIT), pl.ds(SPLIT, ROWS - SPLIT)
    y_below, y_above = (y + 3) % 4, (y + 1) % 4
    x_below, x_above = (x + 3) % 4, (x + 1) % 4
    all_rows, all_cols = pl.ds(0, ROWS), pl.ds(0, PART)
    left, right = pl.ds(0, HEAD), pl.ds(HEAD, HEAD)
    every_y, early, near, far, parts = pl.ds(0, 4), pl.ds(0, 3), pl.ds(1, 2), 3, pl.ds(0, PARTS)

    def z_up(p, places=y, cols=all_cols):
        return send(W.at[p, 0, places, c, all_rows, cols], W.at[p, 1, places, c, all_rows, cols], zp)

    def z_down(p, places=y, cols=all_cols):
        return send(W.at[p, 0, places, c, all_rows, cols], W.at[p, 2, places, c, all_rows, cols], zm)

    def z_on_up(p, places=y, cols=all_cols):
        return send(W.at[p, 1, places, c, A, cols], W.at[p, 3, places, c, A, cols], zp)

    def z_on_down(p, places=y, cols=all_cols):
        return send(W.at[p, 2, places, c, B, cols], W.at[p, 3, places, c, B, cols], zm)

    def y_send(device, p, slots, cols=all_cols):
        block = W.at[p, slots, y, c, all_rows, cols]
        return send(block, block, device)

    def y_on_up(p, slots, cols=all_cols):
        block = W.at[p, slots, y_below, c, low, cols]
        return send(block, block, yp)

    def y_on_down(p, slots, cols=all_cols):
        block = W.at[p, slots, y_above, c, high, cols]
        return send(block, block, ym)

    def x_send(lane, span, device):
        block = X.at[span, x, lane]
        return send(block, block, device)

    def x_on_up(lane):
        block = X.at[0, x_below, lane]
        return send(block, block, xp)

    def x_on_down(lane):
        block = X.at[1, x_above, lane]
        return send(block, block, xm)

    def core_send(p, slots=pl.ds(0, 4), cols=all_cols):
        block = W.at[p, slots, :, c, :, cols]
        return send(block, block, sib)

    def arrive(*copies):
        for copy in copies:
            copy.wait_recv()

    def tables():
        for s in range(2):
            chosen = lax.broadcasted_iota(jnp.int32, (SPANS, HEAD), 0) == span_pos[blk * 2 + s]
            span_cos = jnp.sum(jnp.where(chosen, span_table[0], 0.0), axis=0, keepdims=True)
            span_sin = jnp.sum(jnp.where(chosen, span_table[1], 0.0), axis=0, keepdims=True)
            cosine[s] = (span_cos * row_table[0] - span_sin * row_table[1]).reshape(4, 2, 32, HEAD)
            whole = span_sin * row_table[0] + span_cos * row_table[1]
            lane = lax.broadcasted_iota(jnp.int32, (BLOCK, HEAD), 1)
            sine[s] = jnp.where(lane < HEAD // 2, -whole, whole).reshape(4, 2, 32, HEAD)
        lane = lax.broadcasted_iota(jnp.int32, (HEADS, 2, 4, 2, 32, HEAD), 5)
        span = lax.broadcasted_iota(jnp.int32, (HEADS, 2, 4, 2, 32, HEAD), 1)
        q[:, :, :, :, :, pl.ds(HEAD, HEAD)] = jnp.where(lane == span, 1.0, 0.0).astype(BF16)
        for part in range(2):
            summing[part, :, pl.ds(HEAD, HEAD)] = jnp.ones((4 * BLOCK, HEAD), BF16)

    def project(p, lane):
        total = None
        for slot, place_z in enumerate((z, z_down_at, z_up_at, (z + 2) % 4)):
            depth = pl.ds(pl.multiple_of(place_z * DEPTH, DEPTH), DEPTH)
            rows = X[:, :, pl.ds(lane, 1), :, depth].reshape(BLOCK, DEPTH)
            term = jnp.dot(rows, W[p, slot].reshape(DEPTH, PART), preferred_element_type=F32)
            total = term if total is None else total + term
        return total

    def norm_rotate(raw, gain, lane):
        mean_sq = jnp.mean(raw * raw, axis=-1, keepdims=True)
        normed = raw * lax.rsqrt(mean_sq + EPSILON) * gain
        cos_rows = cosine[:, :, pl.ds(lane, 1)].reshape(BLOCK, HEAD)
        sin_rows = sine[:, :, pl.ds(lane, 1)].reshape(BLOCK, HEAD)
        turned = normed * cos_rows + pltpu.roll(normed, HEAD // 2, 1) * sin_rows
        return turned.astype(BF16).reshape(2, 4, 1, 32, HEAD)

    def keys_values(lane):
        raw = project(0, lane)
        kv[0, :, :, pl.ds(lane, 1), :, pl.ds(0, HEAD)] = norm_rotate(raw[:, :HEAD], key_gain[...], lane)
        kv[0, :, :, pl.ds(lane, 1), :, pl.ds(HEAD, HEAD)] = (
            raw[:, HEAD:].astype(BF16).reshape(2, 4, 1, 32, HEAD))

    def queries(p, lane):
        raw = project(p, lane)
        for j in range(2):
            q[2 * (p - 1) + j, :, :, pl.ds(lane, 1), :, pl.ds(0, HEAD)] = norm_rotate(
                raw[:, j * HEAD:(j + 1) * HEAD], query_gain[...], lane)

    def kv_ahead(lane):
        return send(kv.at[0, :, :, lane], kv.at[2, :, :, lane], nxt)

    def kv_third(lane):
        slot = jnp.where(c == 0, 1, 3)
        return send(kv.at[0, :, :, lane], kv.at[slot, :, :, lane], (third, head))

    def kv_across(lane):
        slot = jnp.where(c == 0, 3, 1)
        return send(kv.at[2, :, :, lane], kv.at[slot, :, :, lane], sib)

    own_pos = [span_pos[blk * 2 + s] for s in range(2)]

    def mask_keys(lane, part):
        column = lax.broadcasted_iota(jnp.int32, (HEAD, HEAD), 1)
        for step in range(4):
            source = (blk + 32 - step) % 32
            for s in range(2):
                pos = span_pos[source * 2 + s]
                hide = [jnp.where(pos <= own_pos[i], 0.0, -MASKED).astype(F32) for i in range(2)]
                masking[part, pl.ds(step * BLOCK + s * HEAD, HEAD), pl.ds(HEAD, HEAD)] = jnp.where(
                    column == 0, hide[0], jnp.where(column == 1, hide[1], 0.0)).astype(BF16)
        key = lax.broadcasted_iota(jnp.int32, (BLOCK, HEAD), 1)
        place_in = key // 32 * 64 + lane * 32 + key % 32
        hidden = jnp.where(lax.broadcasted_iota(jnp.int32, (BLOCK, HEAD), 0) >= place_in, 0.0, -MASKED)
        for i in range(2):
            causal[part, pl.ds(i * BLOCK, BLOCK), pl.ds(i * HEAD, HEAD)] = hidden
            causal[part, pl.ds(i * BLOCK, BLOCK), pl.ds((1 - i) * HEAD, HEAD)] = jnp.zeros((BLOCK, HEAD), F32)

    def gather_keys(lane, part):
        for step in range(4):
            block = kv[step, :, :, pl.ds(lane, 1)].reshape(BLOCK, 2 * HEAD)
            rows = pl.ds(step * BLOCK, BLOCK)
            masking[part, rows, pl.ds(0, HEAD)] = block[:, :HEAD]
            summing[part, rows, pl.ds(0, HEAD)] = block[:, HEAD:]

    factor = HEAD ** (-0.5) * math.log2(math.e)

    def attend(p, half):
        first = half == 0
        for h in (2 * p - 2, 2 * p - 1):
            rows = q[h].reshape(2 * BLOCK, 2 * HEAD)
            peak = None
            found = []
            for step in range(4):
                keys = masking[half, pl.ds(step * BLOCK, BLOCK), :]
                part = lax.dot_general(rows, keys, (((1,), (1,)), ((), ())), preferred_element_type=F32) * factor
                if step == 0:
                    part = part + causal[half]
                found.append(part)
                top = jnp.maximum(part[:, :HEAD], part[:, HEAD:])
                peak = top if peak is None else jnp.maximum(peak, top)
            peak = jnp.max(peak, axis=-1, keepdims=True)
            if first:
                peak = jnp.maximum(peak, LEAST)
            else:
                before_peak = peaks[h][:, 0:1]
                peak = jnp.maximum(peak, before_peak)
            weights = jnp.concatenate([jnp.exp2(part - peak).astype(BF16) for part in found], axis=1)
            summed = jnp.dot(weights, summing[half], preferred_element_type=F32)
            if first:
                partial[h] = summed
                peaks[h] = jnp.broadcast_to(peak, (2 * BLOCK, HEAD))
            else:
                summed = summed + partial[h] * jnp.exp2(before_peak - peak)
                whole = summed[:, HEAD:]
                staged[h] = (summed[:, :HEAD] / whole).reshape(2, BLOCK, HEAD)
                lse = jnp.transpose(peak * math.log(2.0) + jnp.log(whole))
                for i in range(2):
                    log_sum[h, pl.ds(i, 1), :] = lse[0:1, i * BLOCK:(i + 1) * BLOCK]
                pltpu.make_async_copy(staged.at[h], out.at[h], out_sem.at[h]).start()

    z2_p = z_up(2)
    z2_m = z_down(2)
    ya_m = y_send(ym, parts, 0)
    z0_m = z_down(0)
    z0_p = z_up(0)
    lane_b = x_send(l, 1, lp)
    z1_m = z_down(1)
    xo_a_p = x_send(l, 0, xp)
    ya_p = y_send(yp, parts, 0)
    xo_b_m = x_send(l, 1, xm)
    arrive(z2_m)
    z2_fm = z_on_down(2)
    arrive(z2_p)
    y2_p = y_send(yp, 2, near)
    tables()
    mask_keys(l, 0)
    mask_keys(1 - l, 1)
    z2_fp = z_on_up(2)
    xo_a_m = x_send(l, 0, xm)
    z1_p = z_up(1)
    y2_m = y_send(ym, 2, near)
    xo_b_p = x_send(l, 1, xp)
    arrive(z0_p, z0_m)
    y0_m = y_send(ym, 0, near)
    z0_fp = z_on_up(0)
    z0_fm = z_on_down(0)
    arrive(xo_b_m)
    xo_fb = x_on_down(l)
    arrive(ya_m)
    ya_fm = y_on_down(parts, 0)
    y0_p = y_send(yp, 0, near)
    arrive(y2_m)
    y2_fm = y_on_down(2, near)
    arrive(xo_a_p)
    xo_fa = x_on_up(l)
    arrive(y2_p)
    y2_fp = y_on_up(2, near)
    arrive(ya_p)
    ya_fp = y_on_up(parts, 0)
    arrive(lane_b)
    xt_b_p = x_send(1 - l, 1, xp)
    arrive(y0_p)
    y0_fp = y_on_up(0, near)
    lane_a = x_send(l, 0, lp)
    arrive(z1_m)
    z1_fm = z_on_down(1)
    arrive(y0_m)
    y0_fm = y_on_down(0, near)
    arrive(z1_p)
    z1_fp = z_on_up(1)
    arrive(z2_fp, z2_fm)
    y2s_m = y_send(ym, 2, far)
    y2s_p = y_send(yp, 2, far)
    arrive(z0_fp, z0_fm)
    y0s_p = y_send(yp, 0, far)
    z3_p = z_up(3)
    z3_m = z_down(3)
    y0s_m = y_send(ym, 0, far)
    y1_m = y_send(ym, 1, near)
    xt_b_m = x_send(1 - l, 1, xm)
    y1_p = y_send(yp, 1, near)
    zL_m = z_down(4, cols=left)
    arrive(lane_a)
    xt_a_p = x_send(1 - l, 0, xp)
    zL_p = z_up(4, cols=left)
    arrive(y2s_p)
    y2s_fp = y_on_up(2, far)
    xt_a_m = x_send(1 - l, 0, xm)
    arrive(y0s_p)
    y0s_fp = y_on_up(0, far)
    arrive(y2s_m)
    y2s_fm = y_on_down(2, far)
    arrive(y2_fp, y2_fm, ya_fp, ya_fm)
    c2n = core_send(2, early)
    arrive(y0_fp, y0_fm)
    c0n = core_send(0, early)
    arrive(y0s_m)
    y0s_fm = y_on_down(0, far)
    zR_m = z_down(4, every_y, right)
    arrive(z1_fp, z1_fm)
    y1s_m = y_send(ym, 1, far)
    zR_p = z_up(4, every_y, right)
    y1s_p = y_send(yp, 1, far)
    arrive(y1_m)
    y1_fm = y_on_down(1, near)
    arrive(y1_p)
    y1_fp = y_on_up(1, near)
    arrive(y2s_fp, y2s_fm)
    c2f = core_send(2, far)
    arrive(z3_p, z3_m)
    y3_p = y_send(yp, 3, near)
    y3_m = y_send(ym, 3, near)
    arrive(y0s_fp, y0s_fm)
    c0f = core_send(0, far)
    arrive(y1s_m)
    y1s_fm = y_on_down(1, far)
    arrive(y1s_p)
    y1s_fp = y_on_up(1, far)
    arrive(xt_b_m)
    xt_fb = x_on_down(1 - l)
    arrive(zL_m)
    zL_fm = z_on_down(4, cols=left)
    arrive(zL_p)
    yL_p = y_send(yp, 4, near, cols=left)
    arrive(xt_a_p)
    xt_fa = x_on_up(1 - l)
    z3_fm = z_on_down(3)
    zL_fp = z_on_up(4, cols=left)
    yL_m = y_send(ym, 4, near, cols=left)
    arrive(y1_fp, y1_fm)
    c1n = core_send(1, early)
    arrive(c0n, c0f, xo_b_p, xo_a_m, xo_fa, xo_fb)
    keys_values(l)
    z3_fp = z_on_up(3)
    arrive(y3_p)
    y3_fp = y_on_up(3, near)
    knA = kv_ahead(l)
    arrive(y3_m)
    y3_fm = y_on_down(3, near)
    arrive(zR_p)
    zR_fp = z_on_up(4, every_y, right)
    arrive(y1s_fp, y1s_fm)
    c1f = core_send(1, far)
    k3A = kv_third(l)
    arrive(zL_fp, zL_fm)
    yLs_p = y_send(yp, 4, far, cols=left)
    arrive(zR_m)
    zR_fm = z_on_down(4, every_y, right)
    arrive(c2n, c2f)
    queries(2, l)
    arrive(yL_p)
    yL_fp = y_on_up(4, near, cols=left)
    arrive(z3_fp, z3_fm)
    y3s_m = y_send(ym, 3, far)
    yLs_m = y_send(ym, 4, far, cols=left)
    y3s_p = y_send(yp, 3, far)
    arrive(c1n, c1f)
    queries(1, l)
    arrive(xt_b_p, xt_a_m, xt_fa, xt_fb)
    keys_values(1 - l)
    knB = kv_ahead(1 - l)
    k3B = kv_third(1 - l)
    queries(2, 1 - l)
    arrive(y3_fp, y3_fm)
    c3n = core_send(3, early)
    queries(1, 1 - l)
    arrive(yLs_p)
    yLs_fp = y_on_up(4, far, cols=left)
    arrive(y3s_m)
    y3s_fm = y_on_down(3, far)
    arrive(y3s_p)
    y3s_fp = y_on_up(3, far)
    arrive(zR_fp, zR_fm)
    c4b = core_send(4, cols=right)
    arrive(yL_m)
    yL_fm = y_on_down(4, near, cols=left)
    arrive(yLs_m)
    yLs_fm = y_on_down(4, far, cols=left)
    arrive(knA)
    kfA = kv_across(l)
    arrive(k3A, kfA)
    gather_keys(l, 0)
    attend(2, 0)
    attend(1, 0)
    arrive(y3s_fp, y3s_fm)
    c3f = core_send(3, far)
    arrive(yL_fp, yL_fm, yLs_fp, yLs_fm)
    c4a = core_send(4, cols=left)
    arrive(c3n, c3f)
    queries(3, l)
    queries(3, 1 - l)
    arrive(knB)
    kfB = kv_across(1 - l)
    attend(3, 0)
    arrive(c4a, c4b)
    queries(4, l)
    queries(4, 1 - l)
    attend(4, 0)
    arrive(k3B, kfB)
    gather_keys(1 - l, 1)
    attend(2, 1)
    attend(1, 1)
    attend(3, 1)
    attend(4, 1)

    def finish(h, carry):
        pltpu.make_async_copy(staged.at[h], out.at[h], out_sem.at[h]).wait()
        return carry

    lax.fori_loop(0, HEADS, finish, 0)
    for copy in started:
        copy.wait_send()


SENDS = 98


def shards(tokens, span_pos, w_query, key_projection, value_projection, query_gain, key_gain):
    span_table, row_table = rope_tables()
    vmem, anywhere = pl.BlockSpec(memory_space=pltpu.VMEM), pl.BlockSpec(memory_space=pl.ANY)
    hbm = pl.BlockSpec(memory_space=pltpu.HBM)
    return pl.pallas_call(
        kernel,
        out_shape=(
            jax.ShapeDtypeStruct((HEADS, 2, BLOCK, HEAD), F32),
            jax.ShapeDtypeStruct((HEADS, 2, BLOCK), F32),
        ),
        in_specs=[pl.BlockSpec(memory_space=pltpu.SMEM), hbm, hbm, hbm, hbm, vmem, vmem, vmem, vmem],
        out_specs=(anywhere, vmem),
        scratch_shapes=[
            pltpu.VMEM((2, 4, 2, 32, MODEL), BF16),
            pltpu.VMEM((PARTS, 4, 4, 2, ROWS, PART), BF16),
            pltpu.VMEM((4, 2, 4, 2, 32, 2 * HEAD), BF16),
            pltpu.VMEM((HEADS, 2, 4, 2, 32, 2 * HEAD), BF16),
            pltpu.VMEM((2, 4, 2, 32, HEAD), F32),
            pltpu.VMEM((2, 4, 2, 32, HEAD), F32),
            pltpu.VMEM((2, 4 * BLOCK, 2 * HEAD), BF16),
            pltpu.VMEM((2, 4 * BLOCK, 2 * HEAD), BF16),
            pltpu.VMEM((2, 2 * BLOCK, 2 * HEAD), F32),
            pltpu.VMEM((HEADS, 2 * BLOCK, 2 * HEAD), F32),
            pltpu.VMEM((HEADS, 2 * BLOCK, HEAD), F32),
            pltpu.VMEM((HEADS, 2, BLOCK, HEAD), F32),
            pltpu.SemaphoreType.DMA((PARTS + 2,)),
            pltpu.SemaphoreType.DMA((SENDS,)),
            pltpu.SemaphoreType.DMA((SENDS,)),
            pltpu.SemaphoreType.DMA((HEADS,)),
        ],
        compiler_params=pltpu.CompilerParams(
            collective_id=0, has_side_effects=True, vmem_limit_bytes=56 * 2**20),
        name="layer",
    )(span_pos, tokens, w_query, key_projection, value_projection, query_gain[None], key_gain[None],
      span_table, row_table)


def solution(mesh):
    placed = (
        P("blk", "head", None),
        P(),
        P("blk", "head"),
        P("blk", "head"),
        P("blk", "head"),
        P(),
        P(),
    )
    return jax.shard_map(
        shards,
        mesh=mesh,
        in_specs=placed,
        out_specs=(P("head", "blk", None, None), P("head", "blk", None)),
        check_vma=False,
    )
```

```python
import math

import jax
import jax.numpy as jnp
import numpy as np
from jax import lax
from jax.experimental import pallas as pl
from jax.experimental.pallas import tpu as pltpu
from jax.sharding import PartitionSpec as P

MESH = pl.DeviceIdType.MESH
ROPE_BASE = 1000000.0
EPSILON = 1e-06
MASKED = 1e30
LEAST = -1e28
BF16 = jnp.bfloat16
F32 = jnp.float32

MODEL = 5120
HEAD = 128
HEADS = 8
BLOCK = 256
SPANS = 64
ROWS = 160
HALF = 80
SPLIT = 64
PART = 256
PARTS = 5
DEPTH = 8 * ROWS


def rope_tables():
    frequency = ROPE_BASE ** (-(np.arange(HEAD // 2, dtype=np.float64) * 2.0 / HEAD))
    frequency = np.concatenate([frequency, frequency])

    def table(positions):
        angles = positions[:, None].astype(np.float64) * frequency[None, :]
        return np.stack([np.cos(angles), np.sin(angles)]).astype(np.float32)

    return table(np.arange(SPANS) * BLOCK), table(np.arange(BLOCK))


def kernel(
    span_pos, tokens, w_query, w_key, w_value, query_gain, key_gain, span_table, row_table,
    out, log_sum,
    X, W, kv, q, cosine, sine, masking, summing, causal, partial, peaks, staged,
    local_sem, send_sem, recv_sem, out_sem,
):
    blk, head = lax.axis_index("blk"), lax.axis_index("head")
    z, y, c = blk // 8, (blk // 2) % 4, blk % 2
    x, l = head // 2, head % 2
    chip = blk // 2

    def place(z=z, y=y, c=c, x=x, l=l):
        return (z * 8 + y * 2 + c, x * 2 + l)

    z_up_at, z_down_at = (z + 1 + 2 * l) % 4, (z + 3 + 2 * l) % 4
    zp, zm = place(z=z_up_at), place(z=z_down_at)
    yp, ym = place(y=(y + 1) % 4), place(y=(y + 3) % 4)
    xp, xm = place(x=(x + 1) % 4), place(x=(x + 3) % 4)
    lp, sib = place(l=1 - l), place(c=1 - c)
    nxt = (((chip + 1) % 16) * 2 + c, head)
    prv = (((chip + 15) % 16) * 2 + c, head)
    after = (((chip + 2) % 16) * 2, head)
    before = (((chip + 14) % 16) * 2 + 1, head)
    third = jnp.where(c == 0, sib[0], after[0])

    own = [pltpu.make_async_copy(w_key, W.at[0, 0, y, c, :, pl.ds(0, HEAD)], local_sem.at[0]),
           pltpu.make_async_copy(w_value, W.at[0, 0, y, c, :, pl.ds(HEAD, HEAD)], local_sem.at[1])]
    for p in range(1, PARTS):
        own.append(pltpu.make_async_copy(
            w_query.at[:, pl.ds((p - 1) * PART, PART)], W.at[p, 0, y, c], local_sem.at[1 + p]))
    own.append(pltpu.make_async_copy(tokens, X.at[:, x, l], local_sem.at[PARTS + 1]))
    for copy in own:
        copy.start()

    barrier = pltpu.get_barrier_semaphore()
    for device in (zp, zm, yp, ym, xp, xm, lp, sib, prv):
        pl.semaphore_signal(barrier, inc=1, device_id=device, device_id_type=MESH)

    @pl.when(c == 0)
    def _():
        pl.semaphore_signal(barrier, inc=1, device_id=before, device_id_type=MESH)

    pl.semaphore_wait(barrier, 9 + c)
    for copy in own:
        copy.wait()

    started = []

    def send(src, dst, device):
        n = len(started)
        copy = pltpu.make_async_remote_copy(
            src_ref=src, dst_ref=dst, send_sem=send_sem.at[n], recv_sem=recv_sem.at[n],
            device_id=device, device_id_type=MESH)
        copy.start()
        started.append(copy)
        return copy

    A, B = pl.ds(0, HALF), pl.ds(HALF, HALF)
    low, high = pl.ds(0, SPLIT), pl.ds(SPLIT, ROWS - SPLIT)
    y_below, y_above = (y + 3) % 4, (y + 1) % 4
    x_below, x_above = (x + 3) % 4, (x + 1) % 4
    all_rows, all_cols = pl.ds(0, ROWS), pl.ds(0, PART)
    left, right = pl.ds(0, HEAD), pl.ds(HEAD, HEAD)
    every_y, early, near, far, parts = pl.ds(0, 4), pl.ds(0, 3), pl.ds(1, 2), 3, pl.ds(0, PARTS)

    def z_up(p, places=y, cols=all_cols):
        return send(W.at[p, 0, places, c, all_rows, cols], W.at[p, 1, places, c, all_rows, cols], zp)

    def z_down(p, places=y, cols=all_cols):
        return send(W.at[p, 0, places, c, all_rows, cols], W.at[p, 2, places, c, all_rows, cols], zm)

    def z_on_up(p, places=y, cols=all_cols):
        return send(W.at[p, 1, places, c, A, cols], W.at[p, 3, places, c, A, cols], zp)

    def z_on_down(p, places=y, cols=all_cols):
        return send(W.at[p, 2, places, c, B, cols], W.at[p, 3, places, c, B, cols], zm)

    def y_send(device, p, slots, cols=all_cols):
        block = W.at[p, slots, y, c, all_rows, cols]
        return send(block, block, device)

    def y_on_up(p, slots, cols=all_cols):
        block = W.at[p, slots, y_below, c, low, cols]
        return send(block, block, yp)

    def y_on_down(p, slots, cols=all_cols):
        block = W.at[p, slots, y_above, c, high, cols]
        return send(block, block, ym)

    def x_send(lane, span, device):
        block = X.at[span, x, lane]
        return send(block, block, device)

    def x_on_up(lane):
        block = X.at[0, x_below, lane]
        return send(block, block, xp)

    def x_on_down(lane):
        block = X.at[1, x_above, lane]
        return send(block, block, xm)

    def core_send(p, slots=pl.ds(0, 4), cols=all_cols):
        block = W.at[p, slots, :, c, :, cols]
        return send(block, block, sib)

    def arrive(*copies):
        for copy in copies:
            copy.wait_recv()

    def tables():
        for s in range(2):
            chosen = lax.broadcasted_iota(jnp.int32, (SPANS, HEAD), 0) == span_pos[blk * 2 + s]
            span_cos = jnp.sum(jnp.where(chosen, span_table[0], 0.0), axis=0, keepdims=True)
            span_sin = jnp.sum(jnp.where(chosen, span_table[1], 0.0), axis=0, keepdims=True)
            cosine[s] = (span_cos * row_table[0] - span_sin * row_table[1]).reshape(4, 2, 32, HEAD)
            whole = span_sin * row_table[0] + span_cos * row_table[1]
            lane = lax.broadcasted_iota(jnp.int32, (BLOCK, HEAD), 1)
            sine[s] = jnp.where(lane < HEAD // 2, -whole, whole).reshape(4, 2, 32, HEAD)
        lane = lax.broadcasted_iota(jnp.int32, (HEADS, 2, 4, 2, 32, HEAD), 5)
        span = lax.broadcasted_iota(jnp.int32, (HEADS, 2, 4, 2, 32, HEAD), 1)
        q[:, :, :, :, :, pl.ds(HEAD, HEAD)] = jnp.where(lane == span, 1.0, 0.0).astype(BF16)
        for part in range(2):
            summing[part, :, pl.ds(HEAD, HEAD)] = jnp.ones((4 * BLOCK, HEAD), BF16)

    def project(p, lane):
        total = None
        for slot, place_z in enumerate((z, z_down_at, z_up_at, (z + 2) % 4)):
            depth = pl.ds(pl.multiple_of(place_z * DEPTH, DEPTH), DEPTH)
            rows = X[:, :, pl.ds(lane, 1), :, depth].reshape(BLOCK, DEPTH)
            term = jnp.dot(rows, W[p, slot].reshape(DEPTH, PART), preferred_element_type=F32)
            total = term if total is None else total + term
        return total

    def norm_rotate(raw, gain, lane):
        mean_sq = jnp.mean(raw * raw, axis=-1, keepdims=True)
        normed = raw * lax.rsqrt(mean_sq + EPSILON) * gain
        cos_rows = cosine[:, :, pl.ds(lane, 1)].reshape(BLOCK, HEAD)
        sin_rows = sine[:, :, pl.ds(lane, 1)].reshape(BLOCK, HEAD)
        turned = normed * cos_rows + pltpu.roll(normed, HEAD // 2, 1) * sin_rows
        return turned.astype(BF16).reshape(2, 4, 1, 32, HEAD)

    def keys_values(lane):
        raw = project(0, lane)
        kv[0, :, :, pl.ds(lane, 1), :, pl.ds(0, HEAD)] = norm_rotate(raw[:, :HEAD], key_gain[...], lane)
        kv[0, :, :, pl.ds(lane, 1), :, pl.ds(HEAD, HEAD)] = (
            raw[:, HEAD:].astype(BF16).reshape(2, 4, 1, 32, HEAD))

    def queries(p, lane):
        raw = project(p, lane)
        for j in range(2):
            q[2 * (p - 1) + j, :, :, pl.ds(lane, 1), :, pl.ds(0, HEAD)] = norm_rotate(
                raw[:, j * HEAD:(j + 1) * HEAD], query_gain[...], lane)

    def kv_ahead(lane):
        return send(kv.at[0, :, :, lane], kv.at[2, :, :, lane], nxt)

    def kv_third(lane):
        slot = jnp.where(c == 0, 1, 3)
        return send(kv.at[0, :, :, lane], kv.at[slot, :, :, lane], (third, head))

    def kv_across(lane):
        slot = jnp.where(c == 0, 3, 1)
        return send(kv.at[2, :, :, lane], kv.at[slot, :, :, lane], sib)

    own_pos = [span_pos[blk * 2 + s] for s in range(2)]

    def mask_keys(lane, part):
        column = lax.broadcasted_iota(jnp.int32, (HEAD, HEAD), 1)
        for step in range(4):
            source = (blk + 32 - step) % 32
            for s in range(2):
                pos = span_pos[source * 2 + s]
                hide = [jnp.where(pos <= own_pos[i], 0.0, -MASKED).astype(F32) for i in range(2)]
                masking[part, pl.ds(step * BLOCK + s * HEAD, HEAD), pl.ds(HEAD, HEAD)] = jnp.where(
                    column == 0, hide[0], jnp.where(column == 1, hide[1], 0.0)).astype(BF16)
        key = lax.broadcasted_iota(jnp.int32, (BLOCK, HEAD), 1)
        place_in = key // 32 * 64 + lane * 32 + key % 32
        hidden = jnp.where(lax.broadcasted_iota(jnp.int32, (BLOCK, HEAD), 0) >= place_in, 0.0, -MASKED)
        for i in range(2):
            causal[part, pl.ds(i * BLOCK, BLOCK), pl.ds(i * HEAD, HEAD)] = hidden
            causal[part, pl.ds(i * BLOCK, BLOCK), pl.ds((1 - i) * HEAD, HEAD)] = jnp.zeros((BLOCK, HEAD), F32)

    def gather_keys(lane, part):
        for step in range(4):
            block = kv[step, :, :, pl.ds(lane, 1)].reshape(BLOCK, 2 * HEAD)
            rows = pl.ds(step * BLOCK, BLOCK)
            masking[part, rows, pl.ds(0, HEAD)] = block[:, :HEAD]
            summing[part, rows, pl.ds(0, HEAD)] = block[:, HEAD:]

    factor = HEAD ** (-0.5) * math.log2(math.e)

    def attend(p, half):
        first = half == 0
        pair = {}
        for h in (2 * p - 2, 2 * p - 1):
            rows = q[h].reshape(2 * BLOCK, 2 * HEAD)
            peak = None
            found = []
            for step in range(4):
                keys = masking[half, pl.ds(step * BLOCK, BLOCK), :]
                part = lax.dot_general(rows, keys, (((1,), (1,)), ((), ())), preferred_element_type=F32) * factor
                if step == 0:
                    part = part + causal[half]
                found.append(part)
                top = jnp.maximum(part[:, :HEAD], part[:, HEAD:])
                peak = top if peak is None else jnp.maximum(peak, top)
            pair[h] = found, jnp.max(peak, axis=-1, keepdims=True)
        for h, (found, peak) in pair.items():
            if first:
                peak = jnp.maximum(peak, LEAST)
            else:
                before_peak = peaks[h][:, 0:1]
                peak = jnp.maximum(peak, before_peak)
            weights = jnp.concatenate([jnp.exp2(part - peak).astype(BF16) for part in found], axis=1)
            summed = jnp.dot(weights, summing[half], preferred_element_type=F32)
            if first:
                partial[h] = summed
                peaks[h] = jnp.broadcast_to(peak, (2 * BLOCK, HEAD))
            else:
                summed = summed + partial[h] * jnp.exp2(before_peak - peak)
                whole = summed[:, HEAD:]
                staged[h] = (summed[:, :HEAD] / whole).reshape(2, BLOCK, HEAD)
                lse = jnp.transpose(peak * math.log(2.0) + jnp.log(whole))
                for i in range(2):
                    log_sum[h, pl.ds(i, 1), :] = lse[0:1, i * BLOCK:(i + 1) * BLOCK]
                pltpu.make_async_copy(staged.at[h], out.at[h], out_sem.at[h]).start()

    z2_p = z_up(2)
    z2_m = z_down(2)
    ya_m = y_send(ym, parts, 0)
    z0_m = z_down(0)
    z0_p = z_up(0)
    lane_b = x_send(l, 1, lp)
    z1_m = z_down(1)
    xo_a_p = x_send(l, 0, xp)
    ya_p = y_send(yp, parts, 0)
    xo_b_m = x_send(l, 1, xm)
    arrive(z2_m)
    z2_fm = z_on_down(2)
    arrive(z2_p)
    y2_p = y_send(yp, 2, near)
    tables()
    mask_keys(l, 0)
    mask_keys(1 - l, 1)
    z2_fp = z_on_up(2)
    xo_a_m = x_send(l, 0, xm)
    z1_p = z_up(1)
    y2_m = y_send(ym, 2, near)
    xo_b_p = x_send(l, 1, xp)
    arrive(z0_p, z0_m)
    y0_m = y_send(ym, 0, near)
    z0_fp = z_on_up(0)
    z0_fm = z_on_down(0)
    arrive(xo_b_m)
    xo_fb = x_on_down(l)
    arrive(ya_m)
    ya_fm = y_on_down(parts, 0)
    y0_p = y_send(yp, 0, near)
    arrive(y2_m)
    y2_fm = y_on_down(2, near)
    arrive(xo_a_p)
    xo_fa = x_on_up(l)
    arrive(y2_p)
    y2_fp = y_on_up(2, near)
    arrive(ya_p)
    ya_fp = y_on_up(parts, 0)
    arrive(lane_b)
    xt_b_p = x_send(1 - l, 1, xp)
    arrive(y0_p)
    y0_fp = y_on_up(0, near)
    lane_a = x_send(l, 0, lp)
    arrive(z1_m)
    z1_fm = z_on_down(1)
    arrive(y0_m)
    y0_fm = y_on_down(0, near)
    arrive(z1_p)
    z1_fp = z_on_up(1)
    arrive(z2_fp, z2_fm)
    y2s_m = y_send(ym, 2, far)
    y2s_p = y_send(yp, 2, far)
    arrive(z0_fp, z0_fm)
    y0s_p = y_send(yp, 0, far)
    z3_p = z_up(3)
    z3_m = z_down(3)
    y0s_m = y_send(ym, 0, far)
    y1_m = y_send(ym, 1, near)
    xt_b_m = x_send(1 - l, 1, xm)
    y1_p = y_send(yp, 1, near)
    zL_m = z_down(4, cols=left)
    arrive(lane_a)
    xt_a_p = x_send(1 - l, 0, xp)
    zL_p = z_up(4, cols=left)
    arrive(y2s_p)
    y2s_fp = y_on_up(2, far)
    xt_a_m = x_send(1 - l, 0, xm)
    arrive(y0s_p)
    y0s_fp = y_on_up(0, far)
    arrive(y2s_m)
    y2s_fm = y_on_down(2, far)
    arrive(y2_fp, y2_fm, ya_fp, ya_fm)
    c2n = core_send(2, early)
    arrive(y0_fp, y0_fm)
    c0n = core_send(0, early)
    arrive(y0s_m)
    y0s_fm = y_on_down(0, far)
    zR_m = z_down(4, every_y, right)
    arrive(z1_fp, z1_fm)
    y1s_m = y_send(ym, 1, far)
    zR_p = z_up(4, every_y, right)
    y1s_p = y_send(yp, 1, far)
    arrive(y1_m)
    y1_fm = y_on_down(1, near)
    arrive(y1_p)
    y1_fp = y_on_up(1, near)
    arrive(y2s_fp, y2s_fm)
    c2f = core_send(2, far)
    arrive(z3_p, z3_m)
    y3_p = y_send(yp, 3, near)
    y3_m = y_send(ym, 3, near)
    arrive(y0s_fp, y0s_fm)
    c0f = core_send(0, far)
    arrive(y1s_m)
    y1s_fm = y_on_down(1, far)
    arrive(y1s_p)
    y1s_fp = y_on_up(1, far)
    arrive(xt_b_m)
    xt_fb = x_on_down(1 - l)
    arrive(zL_m)
    zL_fm = z_on_down(4, cols=left)
    arrive(zL_p)
    yL_p = y_send(yp, 4, near, cols=left)
    arrive(xt_a_p)
    xt_fa = x_on_up(1 - l)
    z3_fm = z_on_down(3)
    zL_fp = z_on_up(4, cols=left)
    yL_m = y_send(ym, 4, near, cols=left)
    arrive(y1_fp, y1_fm)
    c1n = core_send(1, early)
    arrive(c0n, c0f, xo_b_p, xo_a_m, xo_fa, xo_fb)
    keys_values(l)
    z3_fp = z_on_up(3)
    arrive(y3_p)
    y3_fp = y_on_up(3, near)
    knA = kv_ahead(l)
    arrive(y3_m)
    y3_fm = y_on_down(3, near)
    arrive(zR_p)
    zR_fp = z_on_up(4, every_y, right)
    arrive(y1s_fp, y1s_fm)
    c1f = core_send(1, far)
    k3A = kv_third(l)
    arrive(zL_fp, zL_fm)
    yLs_p = y_send(yp, 4, far, cols=left)
    arrive(zR_m)
    zR_fm = z_on_down(4, every_y, right)
    arrive(c2n, c2f)
    queries(2, l)
    arrive(yL_p)
    yL_fp = y_on_up(4, near, cols=left)
    arrive(z3_fp, z3_fm)
    y3s_m = y_send(ym, 3, far)
    yLs_m = y_send(ym, 4, far, cols=left)
    y3s_p = y_send(yp, 3, far)
    arrive(c1n, c1f)
    queries(1, l)
    arrive(xt_b_p, xt_a_m, xt_fa, xt_fb)
    keys_values(1 - l)
    knB = kv_ahead(1 - l)
    k3B = kv_third(1 - l)
    queries(2, 1 - l)
    arrive(y3_fp, y3_fm)
    c3n = core_send(3, early)
    queries(1, 1 - l)
    arrive(yLs_p)
    yLs_fp = y_on_up(4, far, cols=left)
    arrive(y3s_m)
    y3s_fm = y_on_down(3, far)
    arrive(y3s_p)
    y3s_fp = y_on_up(3, far)
    arrive(zR_fp, zR_fm)
    c4b = core_send(4, cols=right)
    arrive(yL_m)
    yL_fm = y_on_down(4, near, cols=left)
    arrive(yLs_m)
    yLs_fm = y_on_down(4, far, cols=left)
    arrive(knA)
    kfA = kv_across(l)
    arrive(k3A, kfA)
    gather_keys(l, 0)
    attend(2, 0)
    attend(1, 0)
    arrive(y3s_fp, y3s_fm)
    c3f = core_send(3, far)
    arrive(yL_fp, yL_fm, yLs_fp, yLs_fm)
    c4a = core_send(4, cols=left)
    arrive(c3n, c3f)
    queries(3, l)
    queries(3, 1 - l)
    arrive(knB)
    kfB = kv_across(1 - l)
    attend(3, 0)
    arrive(c4a, c4b)
    queries(4, l)
    queries(4, 1 - l)
    attend(4, 0)
    arrive(k3B, kfB)
    gather_keys(1 - l, 1)
    attend(2, 1)
    attend(1, 1)
    attend(3, 1)
    attend(4, 1)

    def finish(h, carry):
        pltpu.make_async_copy(staged.at[h], out.at[h], out_sem.at[h]).wait()
        return carry

    lax.fori_loop(0, HEADS, finish, 0)
    for copy in started:
        copy.wait_send()


SENDS = 98


def shards(tokens, span_pos, w_query, key_projection, value_projection, query_gain, key_gain):
    span_table, row_table = rope_tables()
    vmem, anywhere = pl.BlockSpec(memory_space=pltpu.VMEM), pl.BlockSpec(memory_space=pl.ANY)
    hbm = pl.BlockSpec(memory_space=pltpu.HBM)
    return pl.pallas_call(
        kernel,
        out_shape=(
            jax.ShapeDtypeStruct((HEADS, 2, BLOCK, HEAD), F32),
            jax.ShapeDtypeStruct((HEADS, 2, BLOCK), F32),
        ),
        in_specs=[pl.BlockSpec(memory_space=pltpu.SMEM), hbm, hbm, hbm, hbm, vmem, vmem, vmem, vmem],
        out_specs=(anywhere, vmem),
        scratch_shapes=[
            pltpu.VMEM((2, 4, 2, 32, MODEL), BF16),
            pltpu.VMEM((PARTS, 4, 4, 2, ROWS, PART), BF16),
            pltpu.VMEM((4, 2, 4, 2, 32, 2 * HEAD), BF16),
            pltpu.VMEM((HEADS, 2, 4, 2, 32, 2 * HEAD), BF16),
            pltpu.VMEM((2, 4, 2, 32, HEAD), F32),
            pltpu.VMEM((2, 4, 2, 32, HEAD), F32),
            pltpu.VMEM((2, 4 * BLOCK, 2 * HEAD), BF16),
            pltpu.VMEM((2, 4 * BLOCK, 2 * HEAD), BF16),
            pltpu.VMEM((2, 2 * BLOCK, 2 * HEAD), F32),
            pltpu.VMEM((HEADS, 2 * BLOCK, 2 * HEAD), F32),
            pltpu.VMEM((HEADS, 2 * BLOCK, HEAD), F32),
            pltpu.VMEM((HEADS, 2, BLOCK, HEAD), F32),
            pltpu.SemaphoreType.DMA((PARTS + 2,)),
            pltpu.SemaphoreType.DMA((SENDS,)),
            pltpu.SemaphoreType.DMA((SENDS,)),
            pltpu.SemaphoreType.DMA((HEADS,)),
        ],
        compiler_params=pltpu.CompilerParams(
            collective_id=0, has_side_effects=True, vmem_limit_bytes=56 * 2**20),
        name="layer",
    )(span_pos, tokens, w_query, key_projection, value_projection, query_gain[None], key_gain[None],
      span_table, row_table)


def solution(mesh):
    placed = (
        P("blk", "head", None),
        P(),
        P("blk", "head"),
        P("blk", "head"),
        P("blk", "head"),
        P(),
        P(),
    )
    return jax.shard_map(
        shards,
        mesh=mesh,
        in_specs=placed,
        out_specs=(P("head", "blk", None, None), P("head", "blk", None)),
        check_vma=False,
    )
```
